512 devices in a mesh: owner: 32 (over z, x_hi, core), resp: 16 (over x_lo, y).
Axes of the slice: x: 4 (x_hi: 2, x_lo: 2; x = x_hi * 2 + x_lo), y: 8, z: 8, core: 2. Of those that a mesh axis runs over, the one named last changes fastest.
Arguments:
- queries: bfloat16 [32, 16, 128, 2560], P('owner', 'resp'), may hold values from -8 to 8
- resp_keys: bfloat16 [32, 16, 128, 512], P('owner', 'resp'), may hold values from -8 to 8
- resp_values: bfloat16 [32, 16, 128, 512], P('owner', 'resp'), may hold values from -6 to 6
- out_grad: bfloat16 [32, 16, 128, 2560], P('owner', 'resp'), may hold values from -6 to 6
- prefix_keys: bfloat16 [32, 256, 512], P('owner', 'resp'), may hold values from -6 to 6
- prefix_values: bfloat16 [32, 256, 512], P('owner', 'resp'), may hold values from -6 to 6
- device_prompt: int32 [32, 16], P('owner', 'resp'), may hold values from 0 to 31, as said below
- resp_len: int32 [32, 16], P('owner', 'resp'), may hold values from 32 to 128, as said below
Outputs:
- dquery: bfloat16 [32, 16, 128, 2560], P('owner', 'resp')
- dresp_keys: bfloat16 [32, 16, 128, 512], P('owner', 'resp')
- dresp_values: bfloat16 [32, 16, 128, 512], P('owner', 'resp')
- dprefix_keys: float32 [32, 256, 512], P('owner', 'resp')
- dprefix_values: float32 [32, 256, 512], P('owner', 'resp')
The draws below stay inside these ranges and needn't reach their ends.
Inputs may be any that keep to these rules, and one draw needn't show every extreme that they name: `device_prompt`: A device's prompt is its owner index plus -1, 0 or 1. On every owner index but the first, the device at resp index 0 holds the prompt below; on every owner index but the last, the device at resp index 15 holds the prompt above. `resp_len`: some device holds a response of 128 tokens.
All inputs are finite; a program needn't handle non-finite values.
Results may differ from the reference program's by a relative error of at most 0.0082.
Values may be sent and summed in bfloat16 or wider, within the bound.
A program may use at most 64 MiB of HBM per device.

```python
import math
import jax
import jax.numpy as jnp
from jax import lax

HQ = 20
HK = 4
DH = 128
PRE = 256
RSLOT = 128
N_OWNER = 32
N_RESP = 16


def draw_queries(key, part):
    key = jax.random.fold_in(key, 11)
    values_drawn = jnp.clip(jax.random.normal(key, (N_OWNER, N_RESP, RSLOT, HQ * DH), jnp.float32), -6.0, 6.0)
    return values_drawn.astype(jnp.bfloat16)


def draw_resp_keys(key, part):
    key = jax.random.fold_in(key, 13)
    values_drawn = jnp.clip(jax.random.normal(key, (N_OWNER, N_RESP, RSLOT, HK * DH), jnp.float32), -6.0, 6.0)
    return values_drawn.astype(jnp.bfloat16)


def draw_device_prompt(key, part):
    key = jax.random.fold_in(key, 7)
    offset = jax.random.randint(key, (N_OWNER, N_RESP), -1, 2)
    resp_index = jnp.arange(N_RESP, dtype=jnp.int32)
    offset = jnp.where(resp_index[None, :] == 0, -1, offset)
    offset = jnp.where(resp_index[None, :] == N_RESP - 1, 1, offset)
    owner_index = jnp.arange(N_OWNER, dtype=jnp.int32)
    prompt_index = jnp.clip(owner_index[:, None] + offset, 0, N_OWNER - 1)
    return prompt_index.astype(jnp.int32)


def draw_resp_len(key, part):
    key = jax.random.fold_in(key, 5)
    key_len, key_spot = jax.random.split(key)
    lengths = jax.random.randint(key_len, (N_OWNER * N_RESP,), RSLOT // 4, RSLOT + 1)
    spot_index = jax.random.randint(key_spot, (), 0, N_OWNER * N_RESP)
    lengths = jnp.where(jnp.arange(N_OWNER * N_RESP) == spot_index, RSLOT, lengths)
    return lengths.reshape(N_OWNER, N_RESP).astype(jnp.int32)


def block_scale(own_key, dims, cuts, smallest, largest):
    loudness = 1.0
    for axis_at, parts in cuts:
        heights = jax.random.uniform(jax.random.fold_in(jax.random.fold_in(own_key, 6), axis_at), (parts,), jnp.float32, smallest / len(cuts), largest / len(cuts))
        loudness = loudness * jnp.repeat(jnp.exp(heights), dims[axis_at] // parts).reshape((-1,) + (1,) * (len(dims) - 1 - axis_at))
    return loudness


def scatter_about(rng, shape, width, limit, cuts=(), kind=jnp.bfloat16):
    gain = block_scale(rng, shape, cuts, -0.22, 0.18) if cuts else 1.0
    result = jax.random.normal(rng, shape, jnp.float32) * width * gain
    return jnp.minimum(jnp.maximum(result, -limit), limit).astype(kind)


def setup_inputs(seed: int = 0) -> dict:
    splits = jax.random.split(jax.random.key(seed), 9)
    queries = draw_queries(jax.random.fold_in(splits[8], 71), 0)
    resp_keys = draw_resp_keys(jax.random.fold_in(splits[8], 71), 0)
    resp_values = scatter_about(splits[2], (N_OWNER, N_RESP, RSLOT, HK * DH), 1.0, 6.0, ((0, 32), (1, 16)))
    out_grad = scatter_about(splits[3], (N_OWNER, N_RESP, RSLOT, HQ * DH), 1.0, 6.0, ((0, 32), (1, 16)))
    prefix_keys = scatter_about(splits[4], (N_OWNER, PRE, HK * DH), 1.0, 6.0, ((0, 32), (1, 16)))
    prefix_values = scatter_about(splits[5], (N_OWNER, PRE, HK * DH), 1.0, 6.0, ((0, 32), (1, 16)))
    device_prompt = draw_device_prompt(jax.random.fold_in(splits[8], 71), 0)
    resp_len = draw_resp_len(jax.random.fold_in(splits[8], 71), 0)
    return dict(queries=queries, resp_keys=resp_keys, resp_values=resp_values, out_grad=out_grad, prefix_keys=prefix_keys, prefix_values=prefix_values, device_prompt=device_prompt, resp_len=resp_len)


def rounded(value):
    return lax.optimization_barrier(value.astype(jnp.bfloat16)).astype(jnp.float32)

def response_grads(query_rows, key_rows, value_rows, grad_rows, prefix_k, prefix_v, resp_length):
    score_scale = 1.0 / math.sqrt(DH)
    group_size = HQ // HK
    row_index = jnp.arange(RSLOT, dtype=jnp.int32)
    key_slots = jnp.arange(PRE + RSLOT, dtype=jnp.int32) - PRE
    visible = (key_slots[None, :] < 0) | (key_slots[None, :] <= row_index[:, None]) & (key_slots[None, :] < resp_length)
    valid_rows = (row_index < resp_length).astype(jnp.float32)
    keys_all = jnp.concatenate([prefix_k, key_rows], 0).astype(jnp.float32).reshape(PRE + RSLOT, HK, DH)
    values_all = jnp.concatenate([prefix_v, value_rows], 0).astype(jnp.float32).reshape(PRE + RSLOT, HK, DH)
    query_all = query_rows.astype(jnp.float32).reshape(RSLOT, HK, group_size, DH)
    grad_all = (grad_rows.astype(jnp.float32) * valid_rows[:, None]).reshape(RSLOT, HK, group_size, DH)
    scores = jnp.einsum('rhgd,khd->hgrk', query_all, keys_all) * score_scale
    scores = jnp.where(visible[None, None], scores, jnp.float32(-1e+30))
    row_top = lax.optimization_barrier(jnp.max(scores, -1, keepdims=True))
    exp_terms = jnp.exp(scores - row_top)
    probs = exp_terms / lax.optimization_barrier(jnp.sum(exp_terms, -1, keepdims=True))
    probs_low = rounded(probs)
    output = jnp.einsum('hgrk,khd->rhgd', probs_low, values_all)
    delta = lax.optimization_barrier(jnp.sum(grad_all * output, -1))
    dprobs = jnp.einsum('rhgd,khd->hgrk', grad_all, values_all)
    dscores = rounded(probs * (dprobs - jnp.transpose(delta, (1, 2, 0))[..., None]))
    dquery = jnp.einsum('hgrk,khd->rhgd', dscores, keys_all) * score_scale
    key_grad = (jnp.einsum('hgrk,rhgd->khd', dscores, query_all) * score_scale).reshape(PRE + RSLOT, HK * DH)
    value_grad = jnp.einsum('hgrk,rhgd->khd', probs_low, grad_all).reshape(PRE + RSLOT, HK * DH)
    return (dquery.reshape(RSLOT, HQ * DH).astype(jnp.bfloat16), key_grad[PRE:].astype(jnp.bfloat16), value_grad[PRE:].astype(jnp.bfloat16), key_grad[:PRE], value_grad[:PRE])

def reference(queries, resp_keys, resp_values, out_grad, prefix_keys, prefix_values, device_prompt, resp_len):
    device_count = N_OWNER * N_RESP
    items = (queries.reshape(device_count, RSLOT, HQ * DH), resp_keys.reshape(device_count, RSLOT, HK * DH), resp_values.reshape(device_count, RSLOT, HK * DH), out_grad.reshape(device_count, RSLOT, HQ * DH), device_prompt.reshape(device_count).astype(jnp.int32), resp_len.reshape(device_count).astype(jnp.int32))
    initial = (jnp.zeros((N_OWNER, PRE, HK * DH), jnp.float32), jnp.zeros((N_OWNER, PRE, HK * DH), jnp.float32))

    def visit(running, device_item):
        query_rows, key_rows, value_rows, grad_rows, prompt_index, resp_length = device_item
        prefix_k = lax.dynamic_index_in_dim(prefix_keys, prompt_index, 0, keepdims=False)
        prefix_v = lax.dynamic_index_in_dim(prefix_values, prompt_index, 0, keepdims=False)
        dquery, dkeys, dvalues, dprefix_k, dprefix_v = response_grads(query_rows, key_rows, value_rows, grad_rows, prefix_k, prefix_v, resp_length)
        running = (running[0].at[prompt_index].add(dprefix_k), running[1].at[prompt_index].add(dprefix_v))
        return (running, (dquery, dkeys, dvalues))
    totals, gathered = lax.scan(visit, initial, items)
    return (gathered[0].reshape(N_OWNER, N_RESP, RSLOT, HQ * DH), gathered[1].reshape(N_OWNER, N_RESP, RSLOT, HK * DH), gathered[2].reshape(N_OWNER, N_RESP, RSLOT, HK * DH), totals[0], totals[1])
```

```python
import functools
import math

import jax
import jax.numpy as jnp
from jax import lax
from jax.experimental import pallas as pl
from jax.experimental.pallas import tpu as pltpu
from jax.sharding import PartitionSpec as P

HQ = 20
HK = 4
DH = 128
GROUP = HQ // HK
MESH = pl.DeviceIdType.MESH
F32 = jnp.float32
BF16 = jnp.bfloat16


def dot(a, b, dims):
    return lax.dot_general(a, b, (dims, ((), ())), preferred_element_type=F32)


def slot_weights(tile):
    offset = tile.astype(F32)
    return [jnp.maximum(1.0 - jnp.abs(offset - s), 0.0) for s in (-1.0, 0.0, 1.0)]


def kernel(
    n_owner, n_resp, rows, prefix_len, slots,
    prompt_ref, len_ref, q_hbm, g_hbm, rk_hbm, rv_hbm, pk_hbm, pv_hbm,
    dq_hbm, drk_hbm, drv_hbm, dpk_hbm, dpv_hbm,
    q_all, g_all, kv_all, near, my_tile, tiles, stage, grad_out, grad_in,
    acc, rim_out, rim_in, dq_all, dr_all, dp_all,
    load_sem, near_load_sem, store_sem, near_send, near_recv, tile_send, tile_recv,
    gather_send, gather_recv, grad_send, grad_recv, rim_send, rim_recv,
):
    o = lax.axis_index("owner")
    r = lax.axis_index("resp")
    above = lax.rem(o + 1, n_owner)
    below = lax.rem(o + n_owner - 1, n_owner)
    mine = pl.ds(pl.multiple_of(r * rows, rows), rows)

    def peer(d):
        return lax.rem(r + d, n_resp)

    near_loads = []
    for h in range(HK):
        for kv, ref in enumerate((pk_hbm, pv_hbm)):
            near_loads.append(
                pltpu.make_async_copy(
                    ref.at[:, pl.ds(h * DH, DH)], near.at[1, h, kv], near_load_sem.at[h, kv]
                )
            )
    loads = []
    for h in range(HK):
        for kv, ref in enumerate((rk_hbm, rv_hbm)):
            loads.append(
                pltpu.make_async_copy(
                    ref.at[:, pl.ds(h * DH, DH)],
                    kv_all.at[h, kv, pl.ds(prefix_len, slots)],
                    load_sem.at[len(loads)],
                )
            )
        for g in range(GROUP):
            for ref, target in ((q_hbm, q_all), (g_hbm, g_all)):
                loads.append(
                    pltpu.make_async_copy(
                        ref.at[:, pl.ds((h * GROUP + g) * DH, DH)],
                        target.at[h, pl.ds(g * slots, slots)],
                        load_sem.at[len(loads)],
                    )
                )
    for copy in near_loads:
        copy.start()
    barrier = pltpu.get_barrier_semaphore()
    for target in (above, below):
        pl.semaphore_signal(barrier, inc=1, device_id=(target, r), device_id_type=MESH)

    def greet(d, carry):
        pl.semaphore_signal(barrier, inc=1, device_id=(o, peer(d)), device_id_type=MESH)
        return carry

    lax.fori_loop(1, n_resp, greet, 0)
    for copy in loads:
        copy.start()
    my_tile[...] = jnp.full((rows, DH), (prompt_ref[0, 0] - o).astype(F32)).astype(BF16)
    tiles[r] = my_tile[...]
    for copy in near_loads:
        copy.wait()
    pl.semaphore_wait(barrier, n_resp + 1)

    def near_copy(side):
        return pltpu.make_async_remote_copy(
            src_ref=near.at[1],
            dst_ref=near.at[2 * side],
            send_sem=near_send.at[side],
            recv_sem=near_recv.at[side],
            device_id=((above, below)[side], r),
            device_id_type=MESH,
        )

    def tile_copy(d):
        return pltpu.make_async_remote_copy(
            src_ref=my_tile,
            dst_ref=tiles.at[r],
            send_sem=tile_send.at[d],
            recv_sem=tile_recv.at[d],
            device_id=(o, peer(d)),
            device_id_type=MESH,
        )

    def gather_copy(h, d):
        return pltpu.make_async_remote_copy(
            src_ref=stage.at[h, d],
            dst_ref=kv_all.at[h, :, mine],
            send_sem=gather_send.at[h, d],
            recv_sem=gather_recv.at[h, d],
            device_id=(o, peer(d)),
            device_id_type=MESH,
        )

    def grad_copy(h, d):
        return pltpu.make_async_remote_copy(
            src_ref=grad_out.at[h, peer(d)],
            dst_ref=grad_in.at[h, r],
            send_sem=grad_send.at[h, d],
            recv_sem=grad_recv.at[h, d],
            device_id=(o, peer(d)),
            device_id_type=MESH,
        )

    def rim_copy(h, side):
        return pltpu.make_async_remote_copy(
            src_ref=rim_out.at[h, side],
            dst_ref=rim_in.at[h, side],
            send_sem=rim_send.at[h, side],
            recv_sem=rim_recv.at[h, side],
            device_id=((below, above)[side], r),
            device_id_type=MESH,
        )

    for side in range(2):
        near_copy(side).start()

    def each_peer(action):
        def step(d, carry):
            action(d)
            return carry

        lax.fori_loop(1, n_resp, step, 0)

    each_peer(lambda d: tile_copy(d).start())
    for side in range(2):
        near_copy(side).wait_recv()
    each_peer(lambda d: tile_copy(d).wait_recv())

    def pick(h, tile):
        weights = [w.astype(BF16) for w in slot_weights(tile)]
        return sum(weights[s] * near[s, h] for s in range(3))

    for h in range(HK):

        def send_part(d, h=h):
            stage[h, d] = pick(h, tiles[peer(d)])
            gather_copy(h, d).start()

        each_peer(send_part)
        kv_all[h, :, mine, :] = pick(h, my_tile[...])

    for copy in loads:
        copy.wait()

    length = len_ref[0, 0]
    key_index = lax.broadcasted_iota(jnp.int32, (slots, slots), 0)
    row_index = lax.broadcasted_iota(jnp.int32, (slots, slots), 1)
    hidden = jnp.where((key_index <= row_index) & (key_index < length), 0.0, -1e30)
    hidden = jnp.concatenate([hidden] * GROUP, axis=1)
    valid = jnp.where(key_index < length, 1.0, 0.0).astype(BF16)
    valid = jnp.concatenate([valid] * GROUP, axis=0)
    scale = 1.0 / math.sqrt(DH)
    exp_scale = scale * math.log2(math.e)

    def head(h, carry):
        each_peer(lambda d: gather_copy(h, d).wait_recv())
        keys = kv_all[h, 0]
        values = kv_all[h, 1]
        queries = q_all[h]
        grads = g_all[h] * valid
        scores = dot(keys, queries, ((1,), (1,)))
        scores = jnp.concatenate([scores[:prefix_len], scores[prefix_len:] + hidden], axis=0)
        top = jnp.max(scores, axis=0, keepdims=True)
        terms = jnp.exp2((scores - top) * exp_scale)
        probs = terms * (1.0 / jnp.sum(terms, axis=0, keepdims=True))
        probs_low = probs.astype(BF16)
        dprobs = dot(values, grads, ((1,), (1,)))
        delta = jnp.sum(probs * dprobs, axis=0, keepdims=True)
        dscores = (probs * (dprobs - delta)).astype(BF16)
        dkeys = dot(dscores, queries, ((1,), (0,))) * scale
        dvalues = dot(probs_low, grads, ((1,), (0,)))
        keys_t = keys.astype(F32).T.astype(BF16)
        dquery_t = dot(keys_t, dscores, ((1,), (0,))) * scale
        for kv, value in enumerate((dkeys, dvalues)):
            grad_out[h, :, kv] = value[:prefix_len].astype(BF16).reshape(n_resp, rows, DH)
            dr_all[h, kv] = value[prefix_len:].astype(BF16)
        each_peer(lambda d: grad_copy(h, d).start())
        dq_all[h] = dquery_t.T.astype(BF16)
        grad_in[h, r] = grad_out[h, r]
        return carry

    lax.fori_loop(0, HK, head, 0)

    stores = []
    for h in range(HK):
        for kv, ref in enumerate((drk_hbm, drv_hbm)):
            stores.append(
                pltpu.make_async_copy(
                    dr_all.at[h, kv], ref.at[:, pl.ds(h * DH, DH)], store_sem.at[len(stores)]
                )
            )
        for g in range(GROUP):
            stores.append(
                pltpu.make_async_copy(
                    dq_all.at[h, pl.ds(g * slots, slots)],
                    dq_hbm.at[:, pl.ds((h * GROUP + g) * DH, DH)],
                    store_sem.at[len(stores)],
                )
            )
    for copy in stores:
        copy.start()

    def collect(h, carry):
        each_peer(lambda d: grad_copy(h, d).wait_recv())

        def add(p, sums):
            weights = slot_weights(tiles[p])
            term = grad_in[h, p].astype(F32)
            return tuple(sums[s] + weights[s] * term for s in range(3))

        zero = jnp.zeros((2, rows, DH), F32)
        sums = lax.fori_loop(0, n_resp, add, (zero, zero, zero))
        rim_out[h, 0] = sums[0].astype(BF16)
        rim_out[h, 1] = sums[2].astype(BF16)
        acc[h] = sums[1]
        for side in range(2):
            rim_copy(h, side).start()
        return carry

    lax.fori_loop(0, HK, collect, 0)
    for h in range(HK):
        for side in range(2):
            rim_copy(h, side).wait_recv()
        total = acc[h] + rim_in[h, 0].astype(F32) + rim_in[h, 1].astype(F32)
        dp_all[0, :, pl.ds(h * DH, DH)] = total[0]
        dp_all[1, :, pl.ds(h * DH, DH)] = total[1]
    for kv, ref in enumerate((dpk_hbm, dpv_hbm)):
        copy = pltpu.make_async_copy(dp_all.at[kv], ref, store_sem.at[len(stores)])
        copy.start()
        stores.append(copy)
    for side in range(2):
        near_copy(side).wait_send()
    each_peer(lambda d: tile_copy(d).wait_send())

    def drain(h, carry):
        each_peer(lambda d: gather_copy(h, d).wait_send())
        each_peer(lambda d: grad_copy(h, d).wait_send())
        for side in range(2):
            rim_copy(h, side).wait_send()
        return carry

    lax.fori_loop(0, HK, drain, 0)
    for copy in stores:
        copy.wait()


def body(n_owner, n_resp, queries, resp_keys, resp_values, out_grad, prefix_keys, prefix_values, device_prompt, resp_len):
    slots = queries.shape[2]
    rows = prefix_keys.shape[1]
    prefix_len = rows * n_resp
    total = prefix_len + slots
    anywhere = pl.BlockSpec(memory_space=pl.ANY)
    scalar = pl.BlockSpec(memory_space=pltpu.SMEM)
    dma = pltpu.SemaphoreType.DMA
    vmem = pltpu.VMEM
    flops = 2 * 5 * HQ * slots * total * DH
    outs = pl.pallas_call(
        functools.partial(kernel, n_owner, n_resp, rows, prefix_len, slots),
        out_shape=(
            jax.ShapeDtypeStruct((slots, HQ * DH), BF16),
            jax.ShapeDtypeStruct((slots, HK * DH), BF16),
            jax.ShapeDtypeStruct((slots, HK * DH), BF16),
            jax.ShapeDtypeStruct((rows, HK * DH), F32),
            jax.ShapeDtypeStruct((rows, HK * DH), F32),
        ),
        in_specs=[scalar] * 2 + [anywhere] * 6,
        out_specs=(anywhere,) * 5,
        scratch_shapes=[
            vmem((HK, GROUP * slots, DH), BF16),
            vmem((HK, GROUP * slots, DH), BF16),
            vmem((HK, 2, total, DH), BF16),
            vmem((3, HK, 2, rows, DH), BF16),
            vmem((rows, DH), BF16),
            vmem((n_resp, rows, DH), BF16),
            vmem((HK, n_resp, 2, rows, DH), BF16),
            vmem((HK, n_resp, 2, rows, DH), BF16),
            vmem((HK, n_resp, 2, rows, DH), BF16),
            vmem((HK, 2, rows, DH), F32),
            vmem((HK, 2, 2, rows, DH), BF16),
            vmem((HK, 2, 2, rows, DH), BF16),
            vmem((HK, GROUP * slots, DH), BF16),
            vmem((HK, 2, slots, DH), BF16),
            vmem((2, rows, HK * DH), F32),
            dma((HK * 2 + HQ * 2,)),
            dma((HK, 2)),
            dma((HK * 2 + HQ + 2,)),
            dma((2,)),
            dma((2,)),
            dma((n_resp,)),
            dma((n_resp,)),
            dma((HK, n_resp)),
            dma((HK, n_resp)),
            dma((HK, n_resp)),
            dma((HK, n_resp)),
            dma((HK, 2)),
            dma((HK, 2)),
        ],
        compiler_params=pltpu.CompilerParams(
            collective_id=0, has_side_effects=True, vmem_limit_bytes=40 * 2**20
        ),
        cost_estimate=pl.CostEstimate(flops=flops, bytes_accessed=4 * 2**20, transcendentals=HQ * slots * total),
    )(
        device_prompt, resp_len, queries[0, 0], out_grad[0, 0], resp_keys[0, 0], resp_values[0, 0],
        prefix_keys[0], prefix_values[0],
    )
    dquery, dkeys, dvalues, dprefix_keys, dprefix_values = outs
    return dquery[None, None], dkeys[None, None], dvalues[None, None], dprefix_keys[None], dprefix_values[None]


def solution(mesh):
    row = P("owner", "resp", None, None)
    return jax.shard_map(
        functools.partial(body, mesh.shape["owner"], mesh.shape["resp"]),
        mesh=mesh,
        in_specs=(row, row, row, row, P("owner", "resp", None), P("owner", "resp", None), P("owner", "resp"), P("owner", "resp")),
        out_specs=(row, row, row, P("owner", "resp", None), P("owner", "resp", None)),
        check_vma=False,
    )
```

```python
import functools
import math

import jax
import jax.numpy as jnp
from jax import lax
from jax.experimental import pallas as pl
from jax.experimental.pallas import tpu as pltpu
from jax.sharding import PartitionSpec as P

HQ = 20
HK = 4
DH = 128
GROUP = HQ // HK
MESH = pl.DeviceIdType.MESH
F32 = jnp.float32
BF16 = jnp.bfloat16


def dot(a, b, dims):
    return lax.dot_general(a, b, (dims, ((), ())), preferred_element_type=F32)


def slot_weights(tile):
    offset = tile.astype(F32)
    return [jnp.maximum(1.0 - jnp.abs(offset - s), 0.0) for s in (-1.0, 0.0, 1.0)]


def kernel(
    n_owner, n_resp, rows, prefix_len, slots,
    prompt_ref, len_ref, q_hbm, g_hbm, rk_hbm, rv_hbm, pk_hbm, pv_hbm,
    dq_hbm, drk_hbm, drv_hbm, dpk_hbm, dpv_hbm,
    q_all, g_all, kv_all, near, my_tile, tiles, stage, grad_out, grad_in,
    acc, rim_out, rim_in, dq_all, dr_all, dp_all,
    load_sem, near_load_sem, store_sem, near_send, near_recv, tile_send, tile_recv,
    gather_send, gather_recv, grad_send, grad_recv, rim_send, rim_recv,
):
    o = lax.axis_index("owner")
    r = lax.axis_index("resp")
    above = lax.rem(o + 1, n_owner)
    below = lax.rem(o + n_owner - 1, n_owner)
    mine = pl.ds(pl.multiple_of(r * rows, rows), rows)

    def peer(d):
        return lax.rem(r + d, n_resp)

    near_loads = []
    for h in range(HK):
        for kv, ref in enumerate((pk_hbm, pv_hbm)):
            near_loads.append(
                pltpu.make_async_copy(
                    ref.at[:, pl.ds(h * DH, DH)], near.at[1, h, kv], near_load_sem.at[h, kv]
                )
            )
    loads = []
    for h in range(HK):
        for kv, ref in enumerate((rk_hbm, rv_hbm)):
            loads.append(
                pltpu.make_async_copy(
                    ref.at[:, pl.ds(h * DH, DH)],
                    kv_all.at[h, kv, pl.ds(prefix_len, slots)],
                    load_sem.at[len(loads)],
                )
            )
        for g in range(GROUP):
            for ref, target in ((q_hbm, q_all), (g_hbm, g_all)):
                loads.append(
                    pltpu.make_async_copy(
                        ref.at[:, pl.ds((h * GROUP + g) * DH, DH)],
                        target.at[h, pl.ds(g * slots, slots)],
                        load_sem.at[len(loads)],
                    )
                )
    for copy in near_loads:
        copy.start()
    barrier = pltpu.get_barrier_semaphore()
    for target in (above, below):
        pl.semaphore_signal(barrier, inc=1, device_id=(target, r), device_id_type=MESH)

    def greet(d, carry):
        pl.semaphore_signal(barrier, inc=1, device_id=(o, peer(d)), device_id_type=MESH)
        return carry

    lax.fori_loop(1, n_resp, greet, 0)
    for copy in loads:
        copy.start()
    my_tile[...] = jnp.full((rows, DH), (prompt_ref[0, 0] - o).astype(F32)).astype(BF16)
    tiles[r] = my_tile[...]
    for copy in near_loads:
        copy.wait()
    pl.semaphore_wait(barrier, n_resp + 1)

    def near_copy(side):
        return pltpu.make_async_remote_copy(
            src_ref=near.at[1],
            dst_ref=near.at[2 * side],
            send_sem=near_send.at[side],
            recv_sem=near_recv.at[side],
            device_id=((above, below)[side], r),
            device_id_type=MESH,
        )

    def tile_copy(d):
        return pltpu.make_async_remote_copy(
            src_ref=my_tile,
            dst_ref=tiles.at[r],
            send_sem=tile_send.at[d],
            recv_sem=tile_recv.at[d],
            device_id=(o, peer(d)),
            device_id_type=MESH,
        )

    def gather_copy(h, d):
        return pltpu.make_async_remote_copy(
            src_ref=stage.at[h, d],
            dst_ref=kv_all.at[h, :, mine],
            send_sem=gather_send.at[h, d],
            recv_sem=gather_recv.at[h, d],
            device_id=(o, peer(d)),
            device_id_type=MESH,
        )

    def grad_copy(h, d):
        return pltpu.make_async_remote_copy(
            src_ref=grad_out.at[h, peer(d)],
            dst_ref=grad_in.at[h, r],
            send_sem=grad_send.at[h, d],
            recv_sem=grad_recv.at[h, d],
            device_id=(o, peer(d)),
            device_id_type=MESH,
        )

    def rim_copy(h, side):
        return pltpu.make_async_remote_copy(
            src_ref=rim_out.at[h, side],
            dst_ref=rim_in.at[h, side],
            send_sem=rim_send.at[h, side],
            recv_sem=rim_recv.at[h, side],
            device_id=((below, above)[side], r),
            device_id_type=MESH,
        )

    for side in range(2):
        near_copy(side).start()

    def each_peer(action):
        def step(d, carry):
            action(d)
            return carry

        lax.fori_loop(1, n_resp, step, 0)

    each_peer(lambda d: tile_copy(d).start())
    for side in range(2):
        near_copy(side).wait_recv()
    each_peer(lambda d: tile_copy(d).wait_recv())

    def pick(h, tile):
        weights = [w.astype(BF16) for w in slot_weights(tile)]
        return sum(weights[s] * near[s, h] for s in range(3))

    for h in range(HK):

        def send_part(d, h=h):
            stage[h, d] = pick(h, tiles[peer(d)])
            gather_copy(h, d).start()

        each_peer(send_part)
        kv_all[h, :, mine, :] = pick(h, my_tile[...])

    for copy in loads:
        copy.wait()

    length = len_ref[0, 0]
    key_index = lax.broadcasted_iota(jnp.int32, (slots, slots), 0)
    row_index = lax.broadcasted_iota(jnp.int32, (slots, slots), 1)
    hidden = jnp.where((key_index <= row_index) & (key_index < length), 0.0, -1e30)
    hidden = jnp.concatenate([hidden] * GROUP, axis=1)
    valid = jnp.where(key_index < length, 1.0, 0.0).astype(BF16)
    valid = jnp.concatenate([valid] * GROUP, axis=0)
    scale = 1.0 / math.sqrt(DH)
    exp_scale = scale * math.log2(math.e)

    def head(h, carry):
        each_peer(lambda d: gather_copy(h, d).wait_recv())
        keys = kv_all[h, 0]
        values = kv_all[h, 1]
        queries = q_all[h]
        grads = g_all[h] * valid
        scores = dot(keys, queries, ((1,), (1,)))
        scores = jnp.concatenate([scores[:prefix_len], scores[prefix_len:] + hidden], axis=0)
        top = jnp.max(scores, axis=0, keepdims=True)
        terms = jnp.exp2((scores - top) * exp_scale)
        probs = terms * (1.0 / jnp.sum(terms, axis=0, keepdims=True))
        probs_low = probs.astype(BF16)
        dprobs = dot(values, grads, ((1,), (1,)))
        delta = jnp.sum(probs * dprobs, axis=0, keepdims=True)
        dscores = (probs * (dprobs - delta)).astype(BF16)
        dkeys = dot(dscores, queries, ((1,), (0,))) * scale
        dvalues = dot(probs_low, grads, ((1,), (0,)))
        keys_t = keys.astype(F32).T.astype(BF16)
        dquery_t = dot(keys_t, dscores, ((1,), (0,))) * scale
        for kv, value in enumerate((dkeys, dvalues)):
            grad_out[h, :, kv] = value[:prefix_len].astype(BF16).reshape(n_resp, rows, DH)
            dr_all[h, kv] = value[prefix_len:].astype(BF16)
        each_peer(lambda d: grad_copy(h, d).start())
        dq_all[h] = dquery_t.T.astype(BF16)
        grad_in[h, r] = grad_out[h, r]
        return carry

    lax.fori_loop(0, HK, head, 0)

    stores = []
    for h in range(HK):
        for kv, ref in enumerate((drk_hbm, drv_hbm)):
            stores.append(
                pltpu.make_async_copy(
                    dr_all.at[h, kv], ref.at[:, pl.ds(h * DH, DH)], store_sem.at[len(stores)]
                )
            )
        for g in range(GROUP):
            stores.append(
                pltpu.make_async_copy(
                    dq_all.at[h, pl.ds(g * slots, slots)],
                    dq_hbm.at[:, pl.ds((h * GROUP + g) * DH, DH)],
                    store_sem.at[len(stores)],
                )
            )
    for copy in stores:
        copy.start()

    def collect(h, carry):
        each_peer(lambda d: grad_copy(h, d).wait_recv())

        def add(p, sums):
            weights = slot_weights(tiles[p])
            term = grad_in[h, p].astype(F32)
            return tuple(sums[s] + weights[s] * term for s in range(3))

        zero = jnp.zeros((2, rows, DH), F32)
        sums = lax.fori_loop(0, n_resp, add, (zero, zero, zero))
        rim_out[h, 0] = sums[0].astype(BF16)
        rim_out[h, 1] = sums[2].astype(BF16)
        acc[h] = sums[1]
        for side in range(2):
            rim_copy(h, side).start()
        return carry

    lax.fori_loop(0, HK, collect, 0)
    for h in range(HK):
        for side in range(2):
            rim_copy(h, side).wait_recv()
        total = acc[h] + rim_in[h, 0].astype(F32) + rim_in[h, 1].astype(F32)
        dp_all[0, :, pl.ds(h * DH, DH)] = total[0]
        dp_all[1, :, pl.ds(h * DH, DH)] = total[1]
    for kv, ref in enumerate((dpk_hbm, dpv_hbm)):
        copy = pltpu.make_async_copy(dp_all.at[kv], ref, store_sem.at[len(stores)])
        copy.start()
        stores.append(copy)
    for side in range(2):
        near_copy(side).wait_send()
    each_peer(lambda d: tile_copy(d).wait_send())

    def drain(h, carry):
        each_peer(lambda d: gather_copy(h, d).wait_send())
        each_peer(lambda d: grad_copy(h, d).wait_send())
        for side in range(2):
            rim_copy(h, side).wait_send()
        return carry

    lax.fori_loop(0, HK, drain, 0)
    for copy in stores:
        copy.wait()


def publish(*refs):
    count = len(refs) // 2
    sems = refs[-1]
    copies = [
        pltpu.make_async_copy(refs[i], refs[count + i], sems.at[i]) for i in range(count)
    ]
    for copy in copies:
        copy.start()
    for copy in copies:
        copy.wait()


def body(n_owner, n_resp, queries, resp_keys, resp_values, out_grad, prefix_keys, prefix_values, device_prompt, resp_len):
    slots = queries.shape[2]
    rows = prefix_keys.shape[1]
    prefix_len = rows * n_resp
    total = prefix_len + slots
    anywhere = pl.BlockSpec(memory_space=pl.ANY)
    scalar = pl.BlockSpec(memory_space=pltpu.SMEM)
    dma = pltpu.SemaphoreType.DMA
    vmem = pltpu.VMEM
    flops = 2 * 5 * HQ * slots * total * DH
    outs = pl.pallas_call(
        functools.partial(kernel, n_owner, n_resp, rows, prefix_len, slots),
        out_shape=(
            jax.ShapeDtypeStruct((slots, HQ * DH), BF16),
            jax.ShapeDtypeStruct((slots, HK * DH), BF16),
            jax.ShapeDtypeStruct((slots, HK * DH), BF16),
            jax.ShapeDtypeStruct((rows, HK * DH), F32),
            jax.ShapeDtypeStruct((rows, HK * DH), F32),
        ),
        in_specs=[scalar] * 2 + [anywhere] * 6,
        out_specs=(anywhere,) * 5,
        scratch_shapes=[
            vmem((HK, GROUP * slots, DH), BF16),
            vmem((HK, GROUP * slots, DH), BF16),
            vmem((HK, 2, total, DH), BF16),
            vmem((3, HK, 2, rows, DH), BF16),
            vmem((rows, DH), BF16),
            vmem((n_resp, rows, DH), BF16),
            vmem((HK, n_resp, 2, rows, DH), BF16),
            vmem((HK, n_resp, 2, rows, DH), BF16),
            vmem((HK, n_resp, 2, rows, DH), BF16),
            vmem((HK, 2, rows, DH), F32),
            vmem((HK, 2, 2, rows, DH), BF16),
            vmem((HK, 2, 2, rows, DH), BF16),
            vmem((HK, GROUP * slots, DH), BF16),
            vmem((HK, 2, slots, DH), BF16),
            vmem((2, rows, HK * DH), F32),
            dma((HK * 2 + HQ * 2,)),
            dma((HK, 2)),
            dma((HK * 2 + HQ + 2,)),
            dma((2,)),
            dma((2,)),
            dma((n_resp,)),
            dma((n_resp,)),
            dma((HK, n_resp)),
            dma((HK, n_resp)),
            dma((HK, n_resp)),
            dma((HK, n_resp)),
            dma((HK, 2)),
            dma((HK, 2)),
        ],
        compiler_params=pltpu.CompilerParams(
            collective_id=0, has_side_effects=True, vmem_limit_bytes=63 * 2**20
        ),
        cost_estimate=pl.CostEstimate(flops=flops, bytes_accessed=4 * 2**20, transcendentals=HQ * slots * total),
    )(
        device_prompt, resp_len, queries[0, 0], out_grad[0, 0], resp_keys[0, 0], resp_values[0, 0],
        prefix_keys[0], prefix_values[0],
    )
    dquery, dkeys, dvalues, dprefix_keys, dprefix_values = pl.pallas_call(
        publish,
        out_shape=[jax.ShapeDtypeStruct(x.shape, x.dtype) for x in outs],
        in_specs=[anywhere] * len(outs),
        out_specs=[anywhere] * len(outs),
        scratch_shapes=[dma((len(outs),))],
        compiler_params=pltpu.CompilerParams(vmem_limit_bytes=63 * 2**20),
    )(*outs)
    return dquery[None, None], dkeys[None, None], dvalues[None, None], dprefix_keys[None], dprefix_values[None]


def solution(mesh):
    row = P("owner", "resp", None, None)
    return jax.shard_map(
        functools.partial(body, mesh.shape["owner"], mesh.shape["resp"]),
        mesh=mesh,
        in_specs=(row, row, row, row, P("owner", "resp", None), P("owner", "resp", None), P("owner", "resp"), P("owner", "resp")),
        out_specs=(row, row, row, P("owner", "resp", None), P("owner", "resp", None)),
        check_vma=False,
    )
```

```python
import functools
import math

import jax
import jax.numpy as jnp
from jax import lax
from jax.experimental import pallas as pl
from jax.experimental.pallas import tpu as pltpu
from jax.sharding import PartitionSpec as P

HQ = 20
HK = 4
DH = 128
GROUP = HQ // HK
MESH = pl.DeviceIdType.MESH
F32 = jnp.float32
BF16 = jnp.bfloat16


def dot(a, b, dims):
    return lax.dot_general(a, b, (dims, ((), ())), preferred_element_type=F32)


SLOTS = 4
NY = 8
STEPS = (-1, 3, 1, -3, 4, 0, -2, 2)
KINDS = ((0, 2, 1), (2, 2, -1), (4, 1, None), (5, 3, 0))
PARTS = 2
PER_PART = HK // PARTS


def slot_weights(tile):
    return [jnp.maximum(1.0 - jnp.abs(tile - s), 0.0) for s in range(SLOTS)]


def kernel(
    n_owner, rows, prefix_len, slots,
    prompt_ref, len_ref, q_hbm, g_hbm, rk_hbm, rv_hbm, pk_hbm, pv_hbm,
    dq_hbm, drk_hbm, drv_hbm, dpk_hbm, dpv_hbm,
    q_all, g_all, resp_all, near, tiles, stage, kv_all, grad_out, grad_in,
    sums_out, sums_in, dq_all, dr_all, dp_all,
    load_sem, own_sem, store_sem, near_send, near_recv, tile_send, tile_recv,
    gather_send, gather_recv, grad_send, grad_recv, sums_send, sums_recv,
):
    o = lax.axis_index("owner")
    r = lax.axis_index("resp")
    pairs = n_owner // 2
    k = o // 2
    c = lax.rem(o, 2)
    xl = r // NY
    y = lax.rem(r, NY)
    me = 2 * c + xl
    prompts = (pk_hbm, pv_hbm)
    has_below = k > 0
    has_above = k < pairs - 1
    side = 2 * c - 1
    next_in = (k + side >= 0) & (k + side < pairs)
    other_in = (k - side >= 0) & (k - side < pairs)
    pair_next = lax.rem(k + side + pairs, pairs)
    pair_other = lax.rem(k - side + pairs, pairs)
    pair_below = lax.rem(k + pairs - 1, pairs)
    pair_above = lax.rem(k + 1, pairs)

    y_of = {step: lax.rem(y + (step + NY), NY) for step in (-2, -1, 0, 1, 2)}

    def device(core, x, step):
        return (2 * k + core, x * NY + y_of[step])

    def column(owner, step):
        return (owner, xl * NY + y_of[step])

    def remote(src, dst, send, recv, target):
        return pltpu.make_async_remote_copy(
            src_ref=src, dst_ref=dst, send_sem=send, recv_sem=recv, device_id=target, device_id_type=MESH
        )

    def away(spot):
        return me != spot

    barrier = pltpu.get_barrier_semaphore()

    def signal(target):
        pl.semaphore_signal(barrier, inc=1, device_id=target, device_id_type=MESH)

    for step in (2, -2, 0, 1, -1):
        for spot in range(4):
            if step == 0:
                pl.when(away(spot))(lambda spot=spot: signal(device(spot // 2, spot % 2, 0)))
            else:
                signal(device(spot // 2, spot % 2, step))

    @pl.when(next_in)
    def _():
        for step in (2, -2, 0):
            for kv in range(2):
                signal(column(2 * pair_next + kv, step))

    @pl.when(other_in)
    def _():
        for step in (2, -2, 0):
            signal(column(2 * pair_other + c, step))

    tiles[0, me] = jnp.full((1, DH), (prompt_ref[0, 0] - (2 * k - 1)).astype(F32))

    @pl.when(k == 0)
    def _():
        for where in range(3):
            near[where, 0] = jnp.zeros_like(near[where, 0])

    @pl.when(k == pairs - 1)
    def _():
        for where in range(3):
            near[where, 3] = jnp.zeros_like(near[where, 3])

    @pl.when(jnp.logical_not(next_in))
    def _():
        for where in range(3):
            for kv in range(2):
                sums_in[where, 1, kv] = jnp.zeros_like(sums_in[where, 1, kv])

    own_copies = [pltpu.make_async_copy(prompts[kv], near.at[0, 1 + c], own_sem.at[0]) for kv in range(2)]
    for kv in range(2):
        pl.when(c == kv)(own_copies[kv].start)

    pl.semaphore_wait(barrier, 19 + 6 * next_in.astype(jnp.int32) + 3 * other_in.astype(jnp.int32))

    near_copies = []
    for where, step in ((1, 2), (2, -2), (0, 0)):
        for kind, (pair, slot) in enumerate(((k, 1 + c), (pair_next, 3 - 3 * c))):
            for kv in range(2):
                copy = remote(
                    prompts[kv], near.at[where, slot], near_send.at[where, kind, kv], near_recv.at[where, slot],
                    column(2 * pair + kv, step),
                )
                condition = next_in if kind == 1 else (c != kv if where == 0 else None)
                near_copies.append((condition, copy))

    def tile_copy(spot, step, kind):
        return remote(
            tiles.at[0, me], tiles.at[kind, me], tile_send.at[kind, spot], tile_recv.at[kind, me],
            device(spot // 2, spot % 2, step),
        )

    tile_copies = []
    for kind, step in ((1, -1), (2, 1), (0, 0)):
        for spot in range(4):
            tile_copies.append((away(spot) if kind == 0 else None, tile_copy(spot, step, kind)))
    for core, step in ((0, -2), (1, 2)):
        for spot in range(4):
            tile_copies.append((c == core, tile_copy(spot, step, 3)))

    def each(copies, action):
        for condition, copy in copies:
            if condition is None:
                getattr(copy, action)()
            else:
                pl.when(condition)(getattr(copy, action))

    each(near_copies, "start")
    each(tile_copies, "start")

    loads = [
        pltpu.make_async_copy(rk_hbm, resp_all.at[0], load_sem.at[0]),
        pltpu.make_async_copy(rv_hbm, resp_all.at[1], load_sem.at[1]),
        pltpu.make_async_copy(q_hbm, q_all, load_sem.at[2]),
        pltpu.make_async_copy(g_hbm, g_all, load_sem.at[3]),
    ]

    def arrived(ref, sem):
        remote(ref, ref, near_send.at[0, 0, 0], sem, device(0, 0, 1)).wait_recv()

    for kind in (1, 2, 0, 3):
        for spot in range(4):
            wait = functools.partial(arrived, tiles.at[kind, spot], tile_recv.at[kind, spot])
            if kind == 0:
                pl.when(away(spot))(wait)
            else:
                wait()
    for where in (1, 2, 0):
        for slot in range(SLOTS):
            wait = functools.partial(arrived, near.at[where, slot], near_recv.at[where, slot])
            if slot == 0:
                pl.when(has_below)(wait)
            elif slot == 3:
                pl.when(has_above)(wait)
            elif where == 0:
                pl.when(c != slot - 1)(wait)
            else:
                wait()
    for kv in range(2):
        pl.when(c == kv)(own_copies[kv].wait)

    weights = [[slot_weights(tiles[kind, spot]) for spot in range(4)] for kind in range(4)]

    def gather_copy(part, spot, kind, step):
        first, count, _ = KINDS[kind]
        heads = pl.ds(part * PER_PART, PER_PART)
        blocks = pl.ds(first, count)
        return remote(
            stage.at[heads, spot, blocks], kv_all.at[heads, c, xl, blocks],
            gather_send.at[part, spot, kind], gather_recv.at[part, me, kind], device(spot // 2, spot % 2, step),
        )

    kept = ((1, 2), (2, 1), None, (0, 1, 2))
    gather_copies = []
    for part in range(PARTS):
        block = {}
        for kind, step in ((0, -1), (1, 1), (2, None), (3, 0)):
            first = KINDS[kind][0]
            source = (1, 2, 3, 0)[kind]
            for spot in range(4):
                low = [jnp.broadcast_to(w, (rows, DH)).astype(BF16) for w in weights[{0: 2, 1: 1, 2: 3, 3: 0}[kind]][spot]]
                for j, where in enumerate(kept[kind] or ((1,) if spot < 2 else (2,))):
                    for h in range(part * PER_PART, (part + 1) * PER_PART):
                        columns = slice(h * DH, (h + 1) * DH)
                        stage[h, spot, first + j] = sum(low[s] * near[where, s, :, columns] for s in range(SLOTS))
                copy = gather_copy(part, spot, kind, step if kind != 2 else (2 if spot < 2 else -2))
                condition = away(spot) if kind == 3 else None
                each([(condition, copy)], "start")
                gather_copies.append((condition, copy))
        for h in range(part * PER_PART, (part + 1) * PER_PART):
            kv_all[h, c, xl, 5:8] = stage[h, me, 5:8]
        if part == 0:
            for copy in loads:
                copy.start()

    def gather_arrived(part):
        heads = pl.ds(part * PER_PART, PER_PART)
        for kind, (first, count, _) in enumerate(KINDS):
            for spot in range(4):
                wait = functools.partial(
                    arrived, kv_all.at[heads, spot // 2, spot % 2, pl.ds(first, count)], gather_recv.at[part, spot, kind]
                )
                if kind == 3:
                    pl.when(away(spot))(wait)
                else:
                    wait()

    length = len_ref[0, 0]
    key_index = lax.broadcasted_iota(jnp.int32, (slots, slots), 0)
    row_index = lax.broadcasted_iota(jnp.int32, (slots, slots), 1)
    hidden = jnp.where((key_index <= row_index) & (key_index < length), 0.0, -1e30)
    hidden = jnp.concatenate([hidden] * GROUP, axis=1)
    valid = jnp.where(key_index < length, 1.0, 0.0).astype(BF16)
    scale = 1.0 / math.sqrt(DH)
    exp_scale = scale * math.log2(math.e)

    for copy in loads:
        copy.wait()

    def grad_copies(h):
        copies = []
        for kind, (first, count, step) in enumerate(KINDS):
            blocks = pl.ds(first, count)
            for spot in range(4):
                def make(step, spot=spot, kind=kind, blocks=blocks):
                    return remote(
                        grad_out.at[h, spot // 2, spot % 2, blocks], grad_in.at[h, me, blocks],
                        grad_send.at[h, spot, kind], grad_recv.at[h, me, kind], device(spot // 2, spot % 2, step),
                    )
                if kind == 2:
                    copies.append((c == 0, make(-2)))
                    copies.append((c == 1, make(2)))
                else:
                    copies.append((away(spot) if kind == 3 else None, make(step)))
        return copies

    def sums_copies(first, count):
        heads = pl.ds(first, count)
        part = 0 if first == 0 else 1
        copies = []
        for where, step in ((1, -2), (2, 2), (0, 0)):
            for slot, owner, condition in (
                (0, 2 * pair_below + 1, has_below), (3, 2 * pair_above, has_above), (1, 2 * k, None), (2, 2 * k + 1, None),
            ):
                kind = 1 if slot in (0, 3) else 0
                if where == 0 and kind == 0:
                    condition = c != slot - 1
                copies.append((condition, remote(
                    sums_out.at[where, slot, heads], sums_in.at[where, kind, c, heads],
                    sums_send.at[part, where, slot], sums_recv.at[part, where, kind, c], column(owner, step),
                )))
        return copies

    def combine(h):
        for kind, (first, count, _) in enumerate(KINDS):
            for spot in range(4):
                wait = functools.partial(arrived, grad_in.at[h, spot, pl.ds(first, count)], grad_recv.at[h, spot, kind])
                if kind == 3:
                    pl.when(away(spot))(wait)
                else:
                    wait()
        grad_in[h, me, 5:8] = grad_out[h, c, xl, 5:8]
        below = [(6, 0, s) for s in range(4)] + [(0, 2, s) for s in range(4)] + [(3, 1, s) for s in range(4)] + [(4, 3, 0), (4, 3, 1)]
        above = [(7, 0, s) for s in range(4)] + [(1, 2, s) for s in range(4)] + [(2, 1, s) for s in range(4)] + [(4, 3, 2), (4, 3, 3)]
        here = [(5, 0, s) for s in range(4)]
        for where, terms in enumerate((here, below, above)):
            totals = [None] * SLOTS
            for block, kind, spot in terms:
                piece = grad_in[h, spot, block].astype(F32)
                for s in range(SLOTS):
                    term = weights[kind][spot][s] * piece
                    totals[s] = term if totals[s] is None else totals[s] + term
            for s in range(SLOTS):
                sums_out[where, s, h] = totals[s].astype(BF16)

    def attend(h):
        def columns(ref, first, count=1):
            return ref[:, pl.ds(pl.multiple_of(first, DH), count * DH)]

        keys = jnp.concatenate([kv_all[h, 0].reshape(prefix_len, DH), columns(resp_all.at[0], h * DH)], axis=0)
        values = jnp.concatenate([kv_all[h, 1].reshape(prefix_len, DH), columns(resp_all.at[1], h * DH)], axis=0)
        queries = jnp.concatenate([columns(q_all, (h * GROUP + g) * DH) for g in range(GROUP)], axis=0)
        grads = jnp.concatenate([columns(g_all, (h * GROUP + g) * DH) * valid for g in range(GROUP)], axis=0)
        scores = dot(keys, queries, ((1,), (1,)))
        scores = jnp.concatenate([scores[:prefix_len], scores[prefix_len:] + hidden], axis=0)
        top = jnp.max(scores, axis=0, keepdims=True)
        terms = jnp.exp2((scores - top) * exp_scale)
        probs = terms * (1.0 / jnp.sum(terms, axis=0, keepdims=True))
        probs_low = probs.astype(BF16)
        dprobs = dot(values, grads, ((1,), (1,)))
        delta = jnp.sum(probs * dprobs, axis=0, keepdims=True)
        dscores = (probs * (dprobs - delta)).astype(BF16)
        dkeys = dot(dscores, queries, ((1,), (0,))) * scale
        dvalues = dot(probs_low, grads, ((1,), (0,)))
        for kv, value in enumerate((dkeys, dvalues)):
            grad_out[h, kv] = value[:prefix_len].astype(BF16).reshape(2, NY, rows, DH)
            dr_all[kv, :, pl.ds(pl.multiple_of(h * DH, DH), DH)] = value[prefix_len:].astype(BF16)
        each(grad_copies(h), "start")
        keys_t = keys.astype(F32).T.astype(BF16)
        dquery_t = dot(keys_t, dscores, ((1,), (0,))) * scale
        for g in range(GROUP):
            dquery = dquery_t[:, g * slots:(g + 1) * slots].T.astype(BF16)
            dq_all[:, pl.ds(pl.multiple_of((h * GROUP + g) * DH, DH), DH)] = dquery

    def dq_store(h):
        columns = pl.ds(pl.multiple_of(h * GROUP * DH, DH), GROUP * DH)
        return pltpu.make_async_copy(dq_all.at[:, columns], dq_hbm.at[:, columns], store_sem.at[4 + h])

    def head(h, carry):
        for part in range(PARTS):
            pl.when(h == part * PER_PART)(functools.partial(gather_arrived, part))
        attend(h)
        dq_store(h).start()
        pl.when(h >= 1)(lambda: combine(h - 1))
        return carry

    lax.fori_loop(0, HK, head, 0)
    early = sums_copies(0, HK - 1)
    late = sums_copies(HK - 1, 1)
    each(early, "start")
    stores = [
        pltpu.make_async_copy(dr_all.at[0], drk_hbm, store_sem.at[0]),
        pltpu.make_async_copy(dr_all.at[1], drv_hbm, store_sem.at[1]),
    ]
    for copy in stores:
        copy.start()
    combine(HK - 1)
    each(late, "start")
    sums_in[0, 0, c] = sums_out[0, 1 + c]
    each(near_copies, "wait_send")
    each(tile_copies, "wait_send")
    each(gather_copies, "wait_send")

    for part, heads in enumerate((pl.ds(0, HK - 1), pl.ds(HK - 1, 1))):
        for where in (0, 1, 2):
            for kind in range(2):
                for kv in range(2):
                    wait = functools.partial(
                        arrived, sums_in.at[where, kind, kv, heads], sums_recv.at[part, where, kind, kv]
                    )
                    if kind == 1:
                        pl.when(next_in)(wait)
                    elif where == 0:
                        pl.when(c != kv)(wait)
                    else:
                        wait()
    for kv in range(2):
        for h in range(HK):
            total = jnp.zeros((rows, DH), F32)
            for where in (0, 1, 2):
                for kind in range(2):
                    total += sums_in[where, kind, kv, h].astype(F32)
            dp_all[kv, :, h * DH:(h + 1) * DH] = total
    for kv, ref in enumerate((dpk_hbm, dpv_hbm)):
        copy = pltpu.make_async_copy(dp_all.at[kv], ref, store_sem.at[2 + kv])
        copy.start()
        stores.append(copy)

    each(early, "wait_send")
    each(late, "wait_send")

    def drain(h, carry):
        each(grad_copies(h), "wait_send")
        dq_store(h).wait()
        return carry

    lax.fori_loop(0, HK, drain, 0)
    for copy in stores:
        copy.wait()


def publish(*refs):
    count = (len(refs) - 2) // 3
    ins, outs, held = refs[:count], refs[count:2 * count], refs[2 * count:3 * count]
    in_sem, out_sem = refs[-2:]
    loads = [pltpu.make_async_copy(ins[i], held[i], in_sem.at[i]) for i in range(count)]
    stores = [pltpu.make_async_copy(held[i], outs[i], out_sem.at[i]) for i in range(count)]
    for copy in loads:
        copy.start()
    for i in range(count):
        loads[i].wait()
        stores[i].start()
    for copy in stores:
        copy.wait()


def body(n_owner, n_resp, queries, resp_keys, resp_values, out_grad, prefix_keys, prefix_values, device_prompt, resp_len):
    slots = queries.shape[2]
    rows = prefix_keys.shape[1]
    prefix_len = rows * n_resp
    total = prefix_len + slots
    anywhere = pl.BlockSpec(memory_space=pl.ANY)
    scalar = pl.BlockSpec(memory_space=pltpu.SMEM)
    dma = pltpu.SemaphoreType.DMA
    vmem = pltpu.VMEM
    width = HK * DH
    flops = 2 * 5 * HQ * slots * total * DH
    outs = pl.pallas_call(
        functools.partial(kernel, n_owner, rows, prefix_len, slots),
        out_shape=(
            jax.ShapeDtypeStruct((slots, HQ * DH), BF16),
            jax.ShapeDtypeStruct((slots, width), BF16),
            jax.ShapeDtypeStruct((slots, width), BF16),
            jax.ShapeDtypeStruct((rows, width), F32),
            jax.ShapeDtypeStruct((rows, width), F32),
        ),
        in_specs=[scalar] * 2 + [anywhere] * 6,
        out_specs=(anywhere,) * 5,
        scratch_shapes=[
            vmem((slots, HQ * DH), BF16),
            vmem((slots, HQ * DH), BF16),
            vmem((2, slots, width), BF16),
            vmem((3, SLOTS, rows, width), BF16),
            vmem((4, 4, 1, DH), F32),
            vmem((HK, 4, NY, rows, DH), BF16),
            vmem((HK, 2, 2, NY, rows, DH), BF16),
            vmem((HK, 2, 2, NY, rows, DH), BF16),
            vmem((HK, 4, NY, rows, DH), BF16),
            vmem((3, SLOTS, HK, rows, DH), BF16),
            vmem((3, 2, 2, HK, rows, DH), BF16),
            vmem((slots, HQ * DH), BF16),
            vmem((2, slots, width), BF16),
            vmem((2, rows, width), F32),
            dma((4,)),
            dma((1,)),
            dma((4 + HK,)),
            dma((3, 2, 2)),
            dma((3, SLOTS)),
            dma((4, 4)),
            dma((4, 4)),
            dma((PARTS, 4, 4)),
            dma((PARTS, 4, 4)),
            dma((HK, 4, 4)),
            dma((HK, 4, 4)),
            dma((2, 3, SLOTS)),
            dma((2, 3, 2, 2)),
        ],
        compiler_params=pltpu.CompilerParams(
            collective_id=0, has_side_effects=True, vmem_limit_bytes=63 * 2**20
        ),
        cost_estimate=pl.CostEstimate(flops=flops, bytes_accessed=4 * 2**20, transcendentals=HQ * slots * total),
    )(
        device_prompt, resp_len, queries[0, 0], out_grad[0, 0], resp_keys[0, 0], resp_values[0, 0],
        prefix_keys[0], prefix_values[0],
    )
    dquery, dkeys, dvalues, dprefix_keys, dprefix_values = pl.pallas_call(
        publish,
        out_shape=[jax.ShapeDtypeStruct(x.shape, x.dtype) for x in outs],
        in_specs=[anywhere] * len(outs),
        out_specs=[anywhere] * len(outs),
        scratch_shapes=[vmem(x.shape, x.dtype) for x in outs] + [dma((len(outs),))] * 2,
        compiler_params=pltpu.CompilerParams(vmem_limit_bytes=63 * 2**20),
    )(*outs)
    return dquery[None, None], dkeys[None, None], dvalues[None, None], dprefix_keys[None], dprefix_values[None]


def solution(mesh):
    row = P("owner", "resp", None, None)
    return jax.shard_map(
        functools.partial(body, mesh.shape["owner"], mesh.shape["resp"]),
        mesh=mesh,
        in_specs=(row, row, row, row, P("owner", "resp", None), P("owner", "resp", None), P("owner", "resp"), P("owner", "resp")),
        out_specs=(row, row, row, P("owner", "resp", None), P("owner", "resp", None)),
        check_vma=False,
    )
```

```python
import functools
import math

import jax
import jax.numpy as jnp
from jax import lax
from jax.experimental import pallas as pl
from jax.experimental.pallas import tpu as pltpu
from jax.sharding import PartitionSpec as P

HQ = 20
HK = 4
DH = 128
GROUP = HQ // HK
MESH = pl.DeviceIdType.MESH
F32 = jnp.float32
BF16 = jnp.bfloat16


def dot(a, b, dims):
    return lax.dot_general(a, b, (dims, ((), ())), preferred_element_type=F32)


SLOTS = 4
NY = 8
STEPS = (-1, 3, 1, -3, 4, 0, -2, 2)
KINDS = ((0, 2, 1), (2, 2, -1), (4, 1, None), (5, 3, 0))
PARTS = 2
BANDS = 4
EARLY = 2
PER_PART = HK // PARTS


def slot_weights(tile):
    return [jnp.maximum(1.0 - jnp.abs(tile - s), 0.0) for s in range(SLOTS)]


def kernel(
    n_owner, rows, prefix_len, slots,
    prompt_ref, len_ref, q_hbm, g_hbm, rk_hbm, rv_hbm, pk_hbm, pv_hbm,
    dq_hbm, drk_hbm, drv_hbm, sums_in,
    q_all, g_all, resp_all, near, tiles, stage, kv_all, grad_out, grad_in,
    sums_out, nothing, dq_all, dr_all,
    masked, resp_scores, resp_dprobs, dscores_all,
    store_sem, load_sem, own_sem, near_send, near_recv, tile_send, tile_recv,
    gather_send, gather_recv, grad_send, grad_recv, sums_send, sums_recv,
):
    o = lax.axis_index("owner")
    r = lax.axis_index("resp")
    pairs = n_owner // 2
    k = o // 2
    c = lax.rem(o, 2)
    xl = r // NY
    y = lax.rem(r, NY)
    me = 2 * c + xl
    others = ((1 - c, xl), (c, 1 - xl), (1 - c, 1 - xl))
    prompts = (pk_hbm, pv_hbm)
    has_below = k > 0
    has_above = k < pairs - 1
    side = 2 * c - 1
    next_in = (k + side >= 0) & (k + side < pairs)
    other_in = (k - side >= 0) & (k - side < pairs)
    pair_next = lax.rem(k + side + pairs, pairs)
    pair_other = lax.rem(k - side + pairs, pairs)
    pair_below = lax.rem(k + pairs - 1, pairs)
    pair_above = lax.rem(k + 1, pairs)

    y_of = {step: lax.rem(y + (step + NY), NY) for step in (-2, -1, 0, 1, 2)}
    y_of["far"] = lax.rem(y + (4 * c + NY - 2), NY)

    def device(core, x, step):
        return (2 * k + core, x * NY + y_of[step])

    def column(owner, step):
        return (owner, xl * NY + y_of[step])

    def remote(src, dst, send, recv, target):
        return pltpu.make_async_remote_copy(
            src_ref=src, dst_ref=dst, send_sem=send, recv_sem=recv, device_id=target, device_id_type=MESH
        )

    loads = [
        pltpu.make_async_copy(rk_hbm, resp_all.at[0], load_sem.at[0]),
        pltpu.make_async_copy(rv_hbm, resp_all.at[1], load_sem.at[1]),
        pltpu.make_async_copy(q_hbm, q_all, load_sem.at[2]),
        pltpu.make_async_copy(g_hbm, g_all, load_sem.at[3]),
    ]
    barrier = pltpu.get_barrier_semaphore()

    def signal(target):
        pl.semaphore_signal(barrier, inc=1, device_id=target, device_id_type=MESH)

    for step in (2, -2, 0, 1, -1):
        for spot in range(4):
            if step == 0:
                if spot < 3:
                    signal(device(*others[spot], 0))
            else:
                signal(device(spot // 2, spot % 2, step))

    @pl.when(next_in)
    def _():
        for step in (2, -2, 0):
            for kv in range(2):
                signal(column(2 * pair_next + kv, step))

    @pl.when(other_in)
    def _():
        for step in (2, -2, 0):
            signal(column(2 * pair_other + c, step))

    tiles[0, me] = jnp.full((1, DH), (prompt_ref[0, 0] - (2 * k - 1)).astype(F32))

    blanks = [pltpu.make_async_copy(nothing, sums_in.at[where, 1], store_sem.at[4 + where]) for where in range(3)]

    @pl.when(k == 0)
    def _():
        for where in range(3):
            near[where, 0] = jnp.zeros_like(near[where, 0])

    @pl.when(k == pairs - 1)
    def _():
        for where in range(3):
            near[where, 3] = jnp.zeros_like(near[where, 3])

    @pl.when(jnp.logical_not(next_in))
    def _():
        nothing[...] = jnp.zeros_like(nothing)
        for copy in blanks:
            copy.start()

    own_copies = [pltpu.make_async_copy(prompts[kv], near.at[0, 1 + c], own_sem.at[0]) for kv in range(2)]
    for kv in range(2):
        pl.when(c == kv)(own_copies[kv].start)

    for copy in loads:
        copy.start()
    pl.semaphore_wait(barrier, 19 + 6 * next_in.astype(jnp.int32) + 3 * other_in.astype(jnp.int32))

    def near_copy(where, kind, kv):
        step = {1: 2, 2: -2, 0: 0}[where]
        pair, slot = ((k, 1 + c), (pair_next, 3 - 3 * c))[kind]
        return remote(
            prompts[kv], near.at[where, slot], near_send.at[where, kind, kv], near_recv.at[where, slot],
            column(2 * pair + kv, step),
        )

    def each_near(action):
        @pl.when(next_in)
        def _():
            for where in (1, 2, 0):
                for kv in range(2):
                    getattr(near_copy(where, 1, kv), action)()

        for where in (1, 2):
            for kv in range(2):
                getattr(near_copy(where, 0, kv), action)()
        for kv in range(2):
            pl.when(c != kv)(getattr(near_copy(0, 0, kv), action))

    def tile_copy(core, x, step, kind):
        spot = 2 * core + x
        return remote(
            tiles.at[0, me], tiles.at[kind, me], tile_send.at[kind, spot], tile_recv.at[kind, me], device(core, x, step),
        )

    tile_copies = [
        tile_copy(spot // 2, spot % 2, step, kind) for kind, step in ((1, -1), (2, 1), (3, "far")) for spot in range(4)
    ] + [tile_copy(core, x, 0, 0) for core, x in others]

    def each(copies, action):
        for copy in copies:
            getattr(copy, action)()

    each_near("start")
    each(tile_copies, "start")

    def arrived(ref, sem):
        remote(ref, ref, near_send.at[0, 0, 0], sem, device(0, 0, 1)).wait_recv()

    length = len_ref[0, 0]
    key_index = lax.broadcasted_iota(jnp.int32, (slots, slots), 0)
    row_index = lax.broadcasted_iota(jnp.int32, (slots, slots), 1)
    hidden = jnp.where((key_index <= row_index) & (key_index < length), 0.0, -1e30)
    hidden = jnp.concatenate([hidden] * GROUP, axis=1)
    valid = jnp.where(key_index < length, 1.0, 0.0).astype(BF16)
    scale = 1.0 / math.sqrt(DH)
    exp_scale = scale * math.log2(math.e)

    def columns(ref, first):
        return ref[:, pl.ds(pl.multiple_of(first, DH), DH)]

    def head_queries(h):
        return jnp.concatenate([columns(q_all, (h * GROUP + g) * DH) for g in range(GROUP)], axis=0)

    def prepare(h, carry):
        grads = jnp.concatenate([columns(g_all, (h * GROUP + g) * DH) * valid for g in range(GROUP)], axis=0)
        masked[h] = grads
        resp_scores[h] = dot(columns(resp_all.at[0], h * DH), head_queries(h), ((1,), (1,))) + hidden
        resp_dprobs[h] = dot(columns(resp_all.at[1], h * DH), grads, ((1,), (1,)))
        return carry

    for copy in loads:
        copy.wait()
    lax.fori_loop(0, EARLY, prepare, 0)

    for kind in (1, 2, 3):
        for spot in range(4):
            arrived(tiles.at[kind, spot], tile_recv.at[kind, spot])
    for core, x in others:
        arrived(tiles.at[0, 2 * core + x], tile_recv.at[0, 2 * core + x])

    def near_arrived(where, slot):
        arrived(near.at[where, slot], near_recv.at[where, slot])

    for where in (1, 2):
        near_arrived(where, 1)
        near_arrived(where, 2)
    near_arrived(0, 2 - c)
    for condition, slot in ((has_below, 0), (has_above, 3)):

        @pl.when(condition)
        def _(slot=slot):
            for where in range(3):
                near_arrived(where, slot)

    for kv in range(2):
        pl.when(c == kv)(own_copies[kv].wait)

    weights = [[slot_weights(tiles[kind, spot]) for spot in range(4)] for kind in range(4)]
    weights[0] = [slot_weights(tiles[0, 2 * core + x]) for core, x in others] + [slot_weights(tiles[0, me])]

    def gather_copy(part, spot, kind):
        first, count, _ = KINDS[kind]
        heads = pl.ds(part * PER_PART, PER_PART)
        blocks = pl.ds(first, count)
        if kind == 3:
            target = device(*others[spot], 0)
        else:
            target = device(spot // 2, spot % 2, (-1, 1, 2 if spot < 2 else -2)[kind])
        return remote(
            stage.at[heads, spot, blocks], kv_all.at[heads, c, xl, blocks],
            gather_send.at[part, spot, kind], gather_recv.at[part, me, kind], target,
        )

    gather_copies = []
    for part in range(PARTS):
        for kind in range(4):
            first = KINDS[kind][0]
            for spot in range(4):
                low = [jnp.broadcast_to(w, (rows, DH)).astype(BF16) for w in weights[(2, 1, 3, 0)[kind]][spot]]
                for j, where in enumerate(((1, 2), (2, 1), (1,) if spot < 2 else (2,), (0, 1, 2))[kind]):
                    for h in range(part * PER_PART, (part + 1) * PER_PART):
                        lanes = slice(h * DH, (h + 1) * DH)
                        picked = sum(low[s] * near[where, s, :, lanes] for s in range(SLOTS))
                        if kind == 3 and spot == 3:
                            kv_all[h, c, xl, first + j] = picked
                        else:
                            stage[h, spot, first + j] = picked
                if not (kind == 3 and spot == 3):
                    copy = gather_copy(part, spot, kind)
                    copy.start()
                    gather_copies.append(copy)

    lax.fori_loop(EARLY, HK, prepare, 0)

    def gather_arrived(part):
        heads = pl.ds(part * PER_PART, PER_PART)
        for kind, (first, count, _) in enumerate(KINDS):
            for core, x in others if kind == 3 else ((0, 0), (0, 1), (1, 0), (1, 1)):
                arrived(kv_all.at[heads, core, x, pl.ds(first, count)], gather_recv.at[part, 2 * core + x, kind])

    def grad_copies(h):
        copies = []
        for kind, (first, count, step) in enumerate(KINDS):
            blocks = pl.ds(first, count)
            for core, x in others if kind == 3 else ((0, 0), (0, 1), (1, 0), (1, 1)):
                copies.append(remote(
                    grad_out.at[h, core, x, blocks], grad_in.at[h, me, blocks],
                    grad_send.at[h, 2 * core + x, kind], grad_recv.at[h, me, kind],
                    device(core, x, "far" if kind == 2 else step),
                ))
        return copies

    def each_sum(first, count, action):
        heads = pl.ds(first, count)
        part = 0 if first == 0 else 1

        def act(where, slot, kind, owner):
            copy = remote(
                sums_out.at[where, slot, heads], sums_in.at[where, kind, c, heads],
                sums_send.at[part, where, slot], sums_recv.at[part, where, kind, c],
                column(owner, {1: -2, 2: 2, 0: 0}[where]),
            )
            getattr(copy, action)()

        @pl.when(has_below)
        def _():
            for where in (1, 2, 0):
                act(where, 0, 1, 2 * pair_below + 1)

        @pl.when(has_above)
        def _():
            for where in (1, 2, 0):
                act(where, 3, 1, 2 * pair_above)

        for where in (1, 2):
            act(where, 1, 0, 2 * k)
            act(where, 2, 0, 2 * k + 1)
        act(0, 2 - c, 0, 2 * k + 1 - c)

    def combine(h):
        for kind, (first, count, _) in enumerate(KINDS):
            for core, x in others if kind == 3 else ((0, 0), (0, 1), (1, 0), (1, 1)):
                spot = 2 * core + x
                arrived(grad_in.at[h, spot, pl.ds(first, count)], grad_recv.at[h, spot, kind])

        def piece(block, kind, spot):
            if kind == 0:
                if spot == 3:
                    return grad_out[h, c, xl, block]
                core, x = others[spot]
                return grad_in[h, 2 * core + x, block]
            return grad_in[h, spot, block]

        below = [(6, 0, s) for s in range(4)] + [(0, 2, s) for s in range(4)] + [(3, 1, s) for s in range(4)] + [(4, 3, 0), (4, 3, 1)]
        above = [(7, 0, s) for s in range(4)] + [(1, 2, s) for s in range(4)] + [(2, 1, s) for s in range(4)] + [(4, 3, 2), (4, 3, 3)]
        here = [(5, 0, s) for s in range(4)]
        for where, terms in enumerate((here, below, above)):
            totals = [None] * SLOTS
            for block, kind, spot in terms:
                value = piece(block, kind, spot).astype(F32)
                for s in range(SLOTS):
                    term = weights[kind][spot][s] * value
                    totals[s] = term if totals[s] is None else totals[s] + term
            for s in range(SLOTS):
                sums_out[where, s, h] = totals[s].astype(BF16)

    def attend(h):
        keys = kv_all[h, 0].reshape(prefix_len, DH)
        values = kv_all[h, 1].reshape(prefix_len, DH)
        queries = head_queries(h)
        grads = masked[h]
        scores = jnp.concatenate([dot(keys, queries, ((1,), (1,))), resp_scores[h]], axis=0)
        top = jnp.max(scores, axis=0, keepdims=True)
        terms = jnp.exp2((scores - top) * exp_scale)
        probs = terms * (1.0 / jnp.sum(terms, axis=0, keepdims=True))
        probs_low = probs.astype(BF16)
        dprobs = jnp.concatenate([dot(values, grads, ((1,), (1,))), resp_dprobs[h]], axis=0)
        delta = jnp.sum(probs * dprobs, axis=0, keepdims=True)
        dscores = (probs * (dprobs - delta)).astype(BF16)
        dscores_all[h] = dscores
        dkeys = dot(dscores, queries, ((1,), (0,))) * scale
        dvalues = dot(probs_low, grads, ((1,), (0,)))
        for kv, value in enumerate((dkeys, dvalues)):
            grad_out[h, kv] = value[:prefix_len].astype(BF16).reshape(2, NY, rows, DH)
            dr_all[kv, :, pl.ds(pl.multiple_of(h * DH, DH), DH)] = value[prefix_len:].astype(BF16)
        each(grad_copies(h), "start")

    def query_grads(h, carry):
        keys = jnp.concatenate([kv_all[h, 0].reshape(prefix_len, DH), columns(resp_all.at[0], h * DH)], axis=0)
        keys_t = keys.astype(F32).T.astype(BF16)
        dquery_t = dot(keys_t, dscores_all[h], ((1,), (0,))) * scale
        for g in range(GROUP):
            dquery = dquery_t[:, g * slots:(g + 1) * slots].T.astype(BF16)
            dq_all[:, pl.ds(pl.multiple_of((h * GROUP + g) * DH, DH), DH)] = dquery
        return carry

    def head(h, carry):
        for part in range(PARTS):
            pl.when(h == part * PER_PART)(functools.partial(gather_arrived, part))
        attend(h)
        return carry

    def collect(h, carry):
        combine(h)
        return carry

    lax.fori_loop(0, HK, head, 0)
    stores = [
        pltpu.make_async_copy(held, ref, store_sem.at[i])
        for i, (held, ref) in enumerate((
            (dr_all.at[0], drk_hbm), (dr_all.at[1], drv_hbm), (dq_all, dq_hbm), (sums_out.at[0, 1 + c], sums_in.at[0, 0, c]),
        ))
    ]
    lax.fori_loop(0, HK - 1, collect, 0)
    each_sum(0, HK - 1, "start")
    lax.fori_loop(0, EARLY, query_grads, 0)
    combine(HK - 1)
    each_sum(HK - 1, 1, "start")
    lax.fori_loop(EARLY, HK, query_grads, 0)
    for copy in stores:
        copy.start()
    each_near("wait_send")
    each(tile_copies, "wait_send")
    each(gather_copies, "wait_send")

    def drain(h, carry):
        each(grad_copies(h), "wait_send")
        return carry

    lax.fori_loop(0, HK, drain, 0)

    for part, heads in enumerate((pl.ds(0, HK - 1), pl.ds(HK - 1, 1))):

        def sum_arrived(where, kind, kv):
            arrived(sums_in.at[where, kind, kv, heads], sums_recv.at[part, where, kind, kv])

        sum_arrived(0, 0, 1 - c)
        for where in (1, 2):
            for kv in range(2):
                sum_arrived(where, 0, kv)

        @pl.when(next_in)
        def _():
            for where in range(3):
                for kv in range(2):
                    sum_arrived(where, 1, kv)

    each_sum(0, HK - 1, "wait_send")
    each_sum(HK - 1, 1, "wait_send")
    for copy in stores:
        copy.wait()

    @pl.when(jnp.logical_not(next_in))
    def _():
        for copy in blanks:
            copy.wait()


def publish(
    dq_ref, drk_ref, drv_ref, sums_ref, dq_out, drk_out, drv_out, dpk_out, dpv_out,
    dq, drk, drv, sums, dpk, dpv, in_sem, out_sem,
):
    loads, stores = [], []

    def move(source, held, target):
        sem = len(loads)
        loads.append(pltpu.make_async_copy(source, held, in_sem.at[sem]))
        stores.append(pltpu.make_async_copy(held, target, out_sem.at[sem]))

    sums_load = pltpu.make_async_copy(sums_ref, sums, in_sem.at[BANDS + 2])
    band = dq_ref.shape[0] // BANDS
    for first in range(0, BANDS * band, band):
        span = pl.ds(first, band)
        move(dq_ref.at[span], dq.at[span], dq_out.at[span])
    move(drk_ref, drk, drk_out)
    move(drv_ref, drv, drv_out)
    for copy in loads:
        copy.start()
    sums_load.start()
    for load, store in zip(loads, stores):
        load.wait()
        store.start()
    sums_load.wait()
    for kv, (held, target) in enumerate(((dpk, dpk_out), (dpv, dpv_out))):
        for h in range(HK):
            held[:, h * DH:(h + 1) * DH] = sum(
                sums[where, kind, kv, h].astype(F32) for where in range(3) for kind in range(2)
            )
        copy = pltpu.make_async_copy(held, target, out_sem.at[BANDS + 2 + kv])
        copy.start()
        stores.append(copy)
    for copy in stores:
        copy.wait()


def body(n_owner, n_resp, queries, resp_keys, resp_values, out_grad, prefix_keys, prefix_values, device_prompt, resp_len):
    slots = queries.shape[2]
    rows = prefix_keys.shape[1]
    prefix_len = rows * n_resp
    total = prefix_len + slots
    anywhere = pl.BlockSpec(memory_space=pl.ANY)
    scalar = pl.BlockSpec(memory_space=pltpu.SMEM)
    dma = pltpu.SemaphoreType.DMA
    vmem = pltpu.VMEM
    width = HK * DH
    flops = 2 * 5 * HQ * slots * total * DH
    outs = pl.pallas_call(
        functools.partial(kernel, n_owner, rows, prefix_len, slots),
        out_shape=(
            jax.ShapeDtypeStruct((slots, HQ * DH), BF16),
            jax.ShapeDtypeStruct((slots, width), BF16),
            jax.ShapeDtypeStruct((slots, width), BF16),
            jax.ShapeDtypeStruct((3, 2, 2, HK, rows, DH), BF16),
        ),
        in_specs=[scalar] * 2 + [anywhere] * 6,
        out_specs=(anywhere,) * 4,
        scratch_shapes=[
            vmem((slots, HQ * DH), BF16),
            vmem((slots, HQ * DH), BF16),
            vmem((2, slots, width), BF16),
            vmem((3, SLOTS, rows, width), BF16),
            vmem((4, 4, 1, DH), F32),
            vmem((HK, 4, NY, rows, DH), BF16),
            vmem((HK, 2, 2, NY, rows, DH), BF16),
            vmem((HK, 2, 2, NY, rows, DH), BF16),
            vmem((HK, 4, NY, rows, DH), BF16),
            vmem((3, SLOTS, HK, rows, DH), BF16),
            vmem((2, HK, rows, DH), BF16),
            vmem((slots, HQ * DH), BF16),
            vmem((2, slots, width), BF16),
            vmem((HK, GROUP * slots, DH), BF16),
            vmem((HK, slots, GROUP * slots), F32),
            vmem((HK, slots, GROUP * slots), F32),
            vmem((HK, total, GROUP * slots), BF16),
            dma((7,)),
            dma((4,)),
            dma((1,)),
            dma((3, 2, 2)),
            dma((3, SLOTS)),
            dma((4, 4)),
            dma((4, 4)),
            dma((PARTS, 4, 4)),
            dma((PARTS, 4, 4)),
            dma((HK, 4, 4)),
            dma((HK, 4, 4)),
            dma((2, 3, SLOTS)),
            dma((2, 3, 2, 2)),
        ],
        compiler_params=pltpu.CompilerParams(
            collective_id=0, has_side_effects=True, vmem_limit_bytes=63 * 2**20
        ),
        cost_estimate=pl.CostEstimate(flops=flops, bytes_accessed=4 * 2**20, transcendentals=HQ * slots * total),
    )(
        device_prompt, resp_len, queries[0, 0], out_grad[0, 0], resp_keys[0, 0], resp_values[0, 0],
        prefix_keys[0], prefix_values[0],
    )
    results = [jax.ShapeDtypeStruct(x.shape, x.dtype) for x in outs[:3]] + [jax.ShapeDtypeStruct((rows, width), F32)] * 2
    dquery, dkeys, dvalues, dprefix_keys, dprefix_values = pl.pallas_call(
        publish,
        out_shape=results,
        in_specs=[anywhere] * len(outs),
        out_specs=[anywhere] * len(results),
        scratch_shapes=[vmem(x.shape, x.dtype) for x in (*outs, *results[3:])] + [dma((BANDS + 4,))] * 2,
        compiler_params=pltpu.CompilerParams(vmem_limit_bytes=63 * 2**20),
    )(*outs)
    return dquery[None, None], dkeys[None, None], dvalues[None, None], dprefix_keys[None], dprefix_values[None]


def solution(mesh):
    row = P("owner", "resp", None, None)
    return jax.shard_map(
        functools.partial(body, mesh.shape["owner"], mesh.shape["resp"]),
        mesh=mesh,
        in_specs=(row, row, row, row, P("owner", "resp", None), P("owner", "resp", None), P("owner", "resp"), P("owner", "resp")),
        out_specs=(row, row, row, P("owner", "resp", None), P("owner", "resp", None)),
        check_vma=False,
    )
```
